32 devices in a mesh: row: 4 (over y, x), col: 8 (over z, core).
Axes of the slice: x: 2, y: 2, z: 4, core: 2. Of those that a mesh axis runs over, the one named last changes fastest.
Arguments:
- activations: bfloat16 [32, 10, 28, 1536], P(('row', 'col')), may hold values from -6 to 6
- grad_out: bfloat16 [32, 8, 28, 1536], P(('row', 'col')), may hold values from -6 to 6
- weights: bfloat16 [32, 9, 96, 1536], P(('row', 'col')), may hold values from -6 to 6
- errors: bfloat16 [32, 9, 96, 1536], P(('row', 'col')), may hold values from -4 to 4
- factors: float32 [32, 96, 256], P(('row', 'col')), may hold values from -6 to 6
- step: int32 [], replicated, may hold values from 0 to 99999
- row_offsets: int32 [8], replicated, may hold values from 1 to 2, as said below
- col_offsets: int32 [8], replicated, may hold values from 1 to 4, as said below
Outputs:
- input_grad: bfloat16 [32, 10, 28, 1536], P(('row', 'col'))
- new_weights: bfloat16 [32, 9, 96, 1536], P(('row', 'col'))
- new_errors: bfloat16 [32, 9, 96, 1536], P(('row', 'col'))
- new_factors: float32 [32, 96, 256], P(('row', 'col'))
The draws below stay inside these ranges and needn't reach their ends.
Inputs may be any that keep to these rules, and one draw needn't show every extreme that they name: `row_offsets`: every entry is a power of two. `col_offsets`: every entry is a power of two.
All inputs are finite; a program needn't handle non-finite values.
Results may differ from the reference program's by a relative error of at most 0.001.
Values sent between devices are 32-bit elements; how exact they have to be, the bound alone decides.
A program may use at most 128 MiB of HBM per device.

```python
import math
import jax
import jax.numpy as jnp
from jax import lax

GROUPS = 16
CG = 96
RANK = 16
WIDE = 28
BAND = 8
SCHED = 8
ROW_REPLICAS = 4
COL_REPLICAS = 8
REPLICAS = 32
CHANNELS = 1536


def offset_table(key, replica_count):
    bit_depth = replica_count.bit_length() - 1
    levels = jax.random.randint(key, (SCHED,), 0, bit_depth)
    levels = levels.at[0].set(0).at[1].set(bit_depth - 1)
    levels = jax.random.permutation(jax.random.fold_in(key, 7), levels)
    return jnp.left_shift(jnp.int32(1), levels).astype(jnp.int32)


def draw_row_offsets(key, part):
    return offset_table(jax.random.fold_in(key, 11), ROW_REPLICAS)


def draw_col_offsets(key, part):
    return offset_table(jax.random.fold_in(key, 13), COL_REPLICAS)


def block_scale(rng, dims, cuts, least, largest):
    def one(dim, blocks):
        draws = jax.random.uniform(jax.random.fold_in(jax.random.fold_in(rng, 6), dim), (blocks,), jnp.float32, least / len(cuts), largest / len(cuts))
        return jnp.repeat(jnp.exp(draws), dims[dim] // blocks).reshape((-1,) + (1,) * (len(dims) - dim - 1))

    loudness = one(*cuts[0])
    for cut in cuts[1:]:
        loudness = loudness * one(*cut)
    return loudness


def noise(rng, dims, width, most, cuts=(), kind=jnp.bfloat16):
    values = width * jax.random.normal(rng, dims, jnp.float32)
    if cuts:
        values = values * block_scale(rng, dims, cuts, -0.22, 0.18)
    return jnp.clip(values, -most, most).astype(kind)


def setup_inputs(seed: int = 0) -> dict:
    keys = jax.random.split(jax.random.key(seed), 9)
    return {
        "activations": noise(keys[0], (REPLICAS, BAND + 2, WIDE, CHANNELS), 1.0, 6.0, ((0, 32),)),
        "grad_out": noise(keys[1], (REPLICAS, BAND, WIDE, CHANNELS), 1.0, 6.0, ((0, 32),)),
        "weights": noise(keys[2], (REPLICAS, 9, CG, CHANNELS), 1.0, 6.0, ((0, 32),)),
        "errors": noise(keys[3], (REPLICAS, 9, CG, CHANNELS), 0.25, 4.0, ((0, 32),)),
        "factors": noise(keys[4], (REPLICAS, CG, GROUPS * RANK), 1.0, 6.0, ((0, 32),), jnp.float32),
        "step": jax.random.randint(keys[5], (), 0, 100000).astype(jnp.int32),
        "row_offsets": draw_row_offsets(jax.random.fold_in(keys[8], 71), 0),
        "col_offsets": draw_col_offsets(jax.random.fold_in(keys[8], 71), 0),
    }


LEARN = 0.5
MIXING = 0.5
EPSILON = 1e-06

def backward(inputs, upstream, kernel):
    height = upstream.shape[0]
    breadth = upstream.shape[1]
    weight_scale = 1.0 / math.sqrt(9 * CG)
    padded = jnp.pad(inputs.astype(jnp.float32), ((0, 0), (1, 1), (0, 0))).reshape(height + 2, breadth + 2, GROUPS, CG)
    upward = upstream.astype(jnp.float32).reshape(height, breadth, GROUPS, CG)
    kernels = kernel.astype(jnp.float32).reshape(9, CG, GROUPS, CG)
    shifted = jnp.stack([padded[vertical:vertical + height, lateral:lateral + breadth] for vertical in range(3) for lateral in range(3)])
    gradient = jnp.einsum('thwgc,hwgd->tcgd', shifted, upward, precision=lax.Precision.HIGHEST) * weight_scale
    pieces = jnp.einsum('hwgd,tcgd->thwgc', upward, kernels, precision=lax.Precision.HIGHEST)
    summed = jnp.zeros((height + 2, breadth + 2, GROUPS, CG), jnp.float32)
    for vertical in range(3):
        for lateral in range(3):
            summed = summed + jnp.pad(pieces[3 * vertical + lateral], ((vertical, 2 - vertical), (lateral, 2 - lateral), (0, 0), (0, 0)))
    input_grad = (summed[:, 1:-1] * weight_scale).reshape(height + 2, breadth, GROUPS * CG).astype(jnp.bfloat16)
    return (gradient.reshape(9, CG, GROUPS * CG), input_grad)

def orthonormal(factor):
    columns = []
    for number in range(factor.shape[2]):
        vector = factor[:, :, number]
        for earlier in columns:
            vector = vector - lax.optimization_barrier(jnp.sum(earlier * vector, axis=0)) * earlier
        vector = vector * lax.rsqrt(lax.optimization_barrier(jnp.sum(vector * vector, axis=0)) + EPSILON)
        columns.append(vector)
    return jnp.stack(columns, axis=2)

def reference(activations, grad_out, weights, errors, factors, step, row_offsets, col_offsets):
    position = step % SCHED
    row_offset = row_offsets[position]
    col_offset = col_offsets[position]
    replica = jnp.arange(REPLICAS, dtype=jnp.int32)
    row_index = replica // COL_REPLICAS
    col_index = replica % COL_REPLICAS
    partner = (jnp.bitwise_xor(row_index, row_offset) * COL_REPLICAS + jnp.bitwise_xor(col_index, col_offset)).astype(jnp.int32)
    parity = jnp.where(jnp.bitwise_and(row_index, row_offset) == 0, 1.0, -1.0).astype(jnp.float32)
    warm_start = (factors + factors[partner]) * 0.5

    def project(operands):
        kernel, carried, starting = operands
        merged = (kernel.astype(jnp.float32) + carried.astype(jnp.float32)).reshape(9, CG, GROUPS, CG)
        result = jnp.einsum('tcgd,dgr->tcgr', merged, starting.reshape(CG, GROUPS, RANK), precision=lax.Precision.HIGHEST)
        return result.reshape(9 * CG, GROUPS, RANK)
    sketch = lax.map(project, (weights, errors, warm_start))
    difference = parity[:, None, None, None] * (sketch - sketch[partner])
    subspace = lax.map(orthonormal, difference)

    def transpose_project(operands):
        kernel, carried, basis = operands
        merged = (kernel.astype(jnp.float32) + carried.astype(jnp.float32)).reshape(9 * CG, GROUPS, CG)
        result = jnp.einsum('kgd,kgr->dgr', merged, basis, precision=lax.Precision.HIGHEST)
        return result.reshape(CG, GROUPS * RANK)
    own_proj = lax.map(transpose_project, (weights, errors, subspace))
    next_factors = parity[:, None, None] * (own_proj - own_proj[partner])

    def finish(operands):
        inputs, upstream, kernel, carried, basis, own_part, shared, side = operands
        gradient, input_grad = backward(inputs, upstream, kernel)
        merged = kernel.astype(jnp.float32) + carried.astype(jnp.float32)
        lowrank = jnp.einsum('kgr,dgr->kgd', basis, shared.reshape(CG, GROUPS, RANK), precision=lax.Precision.HIGHEST).reshape(9, CG, GROUPS * CG)
        retained = jnp.einsum('kgr,dgr->kgd', basis, own_part.reshape(CG, GROUPS, RANK), precision=lax.Precision.HIGHEST).reshape(9, CG, GROUPS * CG)
        next_weights = (kernel.astype(jnp.float32) - LEARN * gradient - 0.5 * MIXING * side * lowrank).astype(jnp.bfloat16)
        next_errors = (0.5 * MIXING * (merged - retained)).astype(jnp.bfloat16)
        return (input_grad, next_weights, next_errors)
    input_grads, next_weights, next_errors = lax.map(finish, (activations, grad_out, weights, errors, subspace, own_proj, next_factors, parity))
    return (input_grads, next_weights, next_errors, next_factors)
```

```python
from functools import partial
import math

import jax
import jax.numpy as jnp
from jax import lax
from jax.experimental import pallas as pl
from jax.experimental.pallas import tpu as pltpu
from jax.sharding import PartitionSpec as P

GROUPS = 16
CG = 96
RANK = 16
HALF = 8
HALF_LANES = HALF * CG
QUAD = 4
QUAD_LANES = QUAD * CG
ROWS = 9 * CG
PITCH = 32

LEARN = 0.5
MIXING = 0.5
EPSILON = 1e-06
SCALE = 1.0 / math.sqrt(ROWS)
F32 = jnp.float32
BF16 = jnp.bfloat16
LIMIT = 56 * 1024 * 1024


def thirds(value):
    high = value.astype(BF16)
    rest = value - high.astype(F32)
    middle = rest.astype(BF16)
    low = (rest - middle.astype(F32)).astype(BF16)
    return high, middle, low


def contract(left, right, left_dim, right_dim):
    return lax.dot_general(
        left, right, (((left_dim,), (right_dim,)), ((), ())), preferred_element_type=F32
    )


def lane_group(shape):
    return lax.broadcasted_iota(jnp.int32, shape, len(shape) - 1) // CG


def sketch_kernel(own_ref, weight_ref, error_ref, out_ref):
    spread = own_ref[0].reshape(RANK * HALF, HALF_LANES)
    left = jnp.concatenate(thirds(spread), axis=0)
    total = contract(left, weight_ref[...].reshape(ROWS, HALF_LANES), 1, 1)
    total = total + contract(left, error_ref[...].reshape(ROWS, HALF_LANES), 1, 1)
    count = RANK * HALF
    out_ref[...] = (
        total[:count] + total[count : 2 * count] + total[2 * count :]
    ).reshape(RANK, HALF, ROWS)


def basis_kernel(parity_ref, own_ref, peer_ref, weight_ref, error_ref, basis_ref, proj_ref):
    basis_ref[...] = parity_ref[0] * (own_ref[...] - peer_ref[...])
    for number in range(RANK):
        vector = basis_ref[number]
        norm = jnp.sum(vector * vector, axis=1, keepdims=True)
        vector = vector * lax.rsqrt(norm + EPSILON)
        basis_ref[number] = vector
        for later in range(number + 1, RANK):
            target = basis_ref[later]
            inner = jnp.sum(vector * target, axis=1, keepdims=True)
            basis_ref[later] = target - inner * vector
    count = RANK * HALF
    for half in range(GROUPS // HALF):
        lanes = slice(half * HALF_LANES, (half + 1) * HALF_LANES)
        part = basis_ref[:, half * HALF : (half + 1) * HALF, :].reshape(count, ROWS)
        left = jnp.concatenate(thirds(part), axis=0)
        total = contract(left, weight_ref[:, :, lanes].reshape(ROWS, HALF_LANES), 1, 0)
        total = total + contract(left, error_ref[:, :, lanes].reshape(ROWS, HALF_LANES), 1, 0)
        total = (total[:count] + total[count : 2 * count] + total[2 * count :]).reshape(
            RANK, HALF, HALF_LANES
        )
        own = lane_group((RANK, HALF, HALF_LANES)) == lax.broadcasted_iota(
            jnp.int32, (RANK, HALF, HALF_LANES), 1
        )
        proj_ref[:, lanes] = jnp.sum(jnp.where(own, total, 0.0), axis=1)


def expand(basis, factor):
    count = RANK * HALF
    own = lane_group((RANK, HALF, HALF_LANES)) == lax.broadcasted_iota(
        jnp.int32, (RANK, HALF, HALF_LANES), 1
    )
    spread = jnp.where(own, factor[:, None, :], 0.0).reshape(count, HALF_LANES)
    high, middle, _ = thirds(basis.reshape(count, ROWS))
    spread_high, spread_middle, _ = thirds(spread)
    left = jnp.concatenate([high, high, middle], axis=0)
    right = jnp.concatenate([spread_high, spread_middle, spread_high], axis=0)
    return contract(left, right, 0, 0)


def errors_kernel(basis_ref, proj_ref, weight_ref, error_ref, out_ref):
    retained = expand(basis_ref[...], proj_ref[...]).reshape(9, CG, HALF_LANES)
    merged = weight_ref[...].astype(F32) + error_ref[...].astype(F32)
    out_ref[...] = (0.5 * MIXING * (merged - retained)).astype(BF16)


def weights_kernel(parity_ref, basis_ref, own_ref, peer_ref, base_ref, out_ref, factor_ref):
    factor = parity_ref[0] * (own_ref[...] - peer_ref[...])
    factor_ref[...] = factor
    lowrank = expand(basis_ref[...], factor).reshape(9, CG, HALF_LANES)
    out_ref[...] = (base_ref[...] - 0.5 * MIXING * parity_ref[0] * lowrank).astype(BF16)


def conv_kernel(x_ref, dy_ref, weight_ref, grad_ref, base_ref, x_pad, dy_pad):
    tall, wide, lanes = x_ref.shape
    band = dy_ref.shape[0]
    x_pad[...] = jnp.zeros_like(x_pad)
    dy_pad[...] = jnp.zeros_like(dy_pad)
    x_pad[:, 8 : 8 + wide, :] = x_ref[...].astype(F32)
    dy_pad[:, 8 : 8 + wide, :] = dy_ref[...].astype(F32)
    edge = jnp.zeros((2 * PITCH, lanes), BF16)
    shifted = []
    for lateral in range(3):
        body = dy_pad[:, 9 - lateral : 9 - lateral + PITCH, :].astype(BF16)
        shifted.append(
            jnp.concatenate([edge, body.reshape(band * PITCH, lanes), edge], axis=0)
        )
    count = tall * PITCH

    def lowered(lateral, vertical):
        start = (2 - vertical) * PITCH
        return shifted[lateral][start : start + count]

    upward = jnp.concatenate([lowered(1, vertical) for vertical in range(3)], axis=1)
    groups = lane_group((CG, lanes))
    for lateral in range(3):
        window = x_pad[:, 7 + lateral : 7 + lateral + PITCH, :].astype(BF16)
        result = contract(window.reshape(count, lanes), upward, 0, 0)
        for vertical in range(3):
            tap = 3 * vertical + lateral
            columns = slice(vertical * lanes, (vertical + 1) * lanes)
            gradient = result[:CG, columns]
            for group in range(1, QUAD):
                gradient = jnp.where(
                    groups == group, result[group * CG : (group + 1) * CG, columns], gradient
                )
            base_ref[tap] = weight_ref[tap].astype(F32) - (LEARN * SCALE) * gradient
    total = jnp.zeros((count, lanes), F32)
    zero = jnp.zeros((CG, lanes), BF16)
    for vertical in range(3):
        for lateral in range(3):
            kernel = weight_ref[3 * vertical + lateral]
            blocked = jnp.concatenate(
                [jnp.where(groups == group, kernel, zero) for group in range(QUAD)], axis=0
            )
            total = total + contract(lowered(lateral, vertical), blocked, 1, 1)
    grad_ref[...] = (total * SCALE).reshape(tall, PITCH, lanes)[:, :wide, :].astype(BF16)


def params():
    return pltpu.CompilerParams(vmem_limit_bytes=LIMIT)


SCALAR = pl.BlockSpec(memory_space=pltpu.SMEM)
WHOLE = pl.BlockSpec(memory_space=pltpu.VMEM)
TAPS = pl.BlockSpec((9, CG, HALF_LANES), lambda i: (0, 0, i))
BASIS = pl.BlockSpec((RANK, HALF, ROWS), lambda i: (0, i, 0))
THIN = pl.BlockSpec((RANK, HALF_LANES), lambda i: (0, i))


def sketch_of(spread, weights, errors):
    return pl.pallas_call(
        sketch_kernel,
        grid=(GROUPS // HALF,),
        in_specs=[
            pl.BlockSpec((1, RANK, HALF, HALF_LANES), lambda i: (i, 0, 0, 0)),
            TAPS,
            TAPS,
        ],
        out_specs=BASIS,
        out_shape=jax.ShapeDtypeStruct((RANK, GROUPS, ROWS), F32),
        compiler_params=params(),
    )(spread, weights, errors)


def basis_of(parity, own, peer, weights, errors):
    return pl.pallas_call(
        basis_kernel,
        in_specs=[SCALAR, WHOLE, WHOLE, WHOLE, WHOLE],
        out_specs=(WHOLE, WHOLE),
        out_shape=(
            jax.ShapeDtypeStruct((RANK, GROUPS, ROWS), F32),
            jax.ShapeDtypeStruct((RANK, GROUPS * CG), F32),
        ),
        compiler_params=params(),
    )(parity, own, peer, weights, errors)


def errors_of(basis, proj, weights, errors):
    return pl.pallas_call(
        errors_kernel,
        grid=(GROUPS // HALF,),
        in_specs=[BASIS, THIN, TAPS, TAPS],
        out_specs=TAPS,
        out_shape=jax.ShapeDtypeStruct(errors.shape, BF16),
        compiler_params=params(),
        cost_estimate=pl.CostEstimate(
            flops=4 * 10**9, bytes_accessed=10 * 10**6, transcendentals=0
        ),
    )(basis, proj, weights, errors)


def weights_of(parity, basis, own, peer, base):
    return pl.pallas_call(
        weights_kernel,
        grid=(GROUPS // HALF,),
        in_specs=[SCALAR, BASIS, THIN, THIN, TAPS],
        out_specs=(TAPS, THIN),
        out_shape=(
            jax.ShapeDtypeStruct(base.shape, BF16),
            jax.ShapeDtypeStruct(own.shape, F32),
        ),
        compiler_params=params(),
    )(parity, basis, own, peer, base)


def conv_of(activations, upstream, weights):
    def banded(rows, wide):
        return pl.BlockSpec((rows, wide, QUAD_LANES), lambda i: (0, 0, i))

    tall, wide, _ = activations.shape
    band = upstream.shape[0]
    taps = pl.BlockSpec((9, CG, QUAD_LANES), lambda i: (0, 0, i))
    return pl.pallas_call(
        conv_kernel,
        grid=(GROUPS // QUAD,),
        in_specs=[banded(tall, wide), banded(band, wide), taps],
        out_specs=(banded(tall, wide), taps),
        out_shape=(
            jax.ShapeDtypeStruct(activations.shape, BF16),
            jax.ShapeDtypeStruct(weights.shape, F32),
        ),
        scratch_shapes=[
            pltpu.VMEM((tall, PITCH + 16, QUAD_LANES), F32),
            pltpu.VMEM((band, PITCH + 16, QUAD_LANES), F32),
        ],
        compiler_params=params(),
        cost_estimate=pl.CostEstimate(
            flops=16 * 10**9, bytes_accessed=12 * 10**6, transcendentals=0
        ),
    )(activations, upstream, weights)


def level_of(offset, bit_count):
    powers = jnp.left_shift(jnp.int32(1), jnp.arange(bit_count, dtype=jnp.int32))
    return jnp.sum((powers < offset).astype(jnp.int32))


def paired(value, row_bit, col_bit):
    rows, cols = lax.axis_size("row"), lax.axis_size("col")
    pairs = [
        (r * cols + c, (r ^ (1 << row_bit)) * cols + (c ^ (1 << col_bit)))
        for r in range(rows)
        for c in range(cols)
    ]
    return lax.ppermute(value, ("row", "col"), pairs)


def local(activations, grad_out, weights, errors, factors, step, row_offsets, col_offsets):
    row_bits = lax.axis_size("row").bit_length() - 1
    col_bits = lax.axis_size("col").bit_length() - 1
    position = step % row_offsets.shape[0]
    row_offset = row_offsets[position]
    col_offset = col_offsets[position]
    level = level_of(row_offset, row_bits) * col_bits + level_of(col_offset, col_bits)
    parity = jnp.where(jnp.bitwise_and(lax.axis_index("row"), row_offset) == 0, 1.0, -1.0)
    parity = parity.astype(F32).reshape(1)

    def across(work, *operands):
        branches = [
            partial(work, lambda value, r=r, c=c: paired(value, r, c))
            for r in range(row_bits)
            for c in range(col_bits)
        ]
        return lax.switch(level, branches, *operands)

    taps, carried = weights[0], errors[0]
    own_factor = factors[0]
    peer_factor = across(lambda send, value: send(value), own_factor)
    warm = ((own_factor + peer_factor) * 0.5).reshape(CG, GROUPS // HALF, HALF, RANK)
    warm = warm.transpose(1, 3, 2, 0)
    eye = jnp.eye(HALF, dtype=F32)
    spread = (warm[:, :, :, None, :] * eye[None, None, :, :, None]).reshape(
        GROUPS // HALF, RANK, HALF, HALF_LANES
    )
    sketch = sketch_of(spread, taps, carried)

    def swap_sketch(send, value, inputs, upstream, kernel):
        return send(value), conv_of(inputs, upstream, kernel)

    remote, (input_grad, base) = across(
        swap_sketch, sketch, activations[0], grad_out[0], taps
    )
    basis, own_proj = basis_of(parity, sketch, remote, taps, carried)

    def swap_proj(send, value, basis, kernel, carried):
        return send(value), errors_of(basis, value, kernel, carried)

    peer_proj, next_errors = across(swap_proj, own_proj, basis, taps, carried)
    next_weights, next_thin = weights_of(parity, basis, own_proj, peer_proj, base)
    next_factor = next_thin.reshape(RANK, GROUPS, CG).transpose(2, 1, 0).reshape(factors.shape)
    return (input_grad[None], next_weights[None], next_errors[None], next_factor)


def solution(mesh):
    placed = (
        P(("row", "col"), None, None, None),
        P(("row", "col"), None, None, None),
        P(("row", "col"), None, None, None),
        P(("row", "col"), None, None, None),
        P(("row", "col"), None, None),
        P(),
        P(),
        P(),
    )
    return jax.shard_map(
        local,
        mesh=mesh,
        in_specs=placed,
        out_specs=(
            P(("row", "col"), None, None, None),
            P(("row", "col"), None, None, None),
            P(("row", "col"), None, None, None),
            P(("row", "col"), None, None),
        ),
        check_vma=False,
    )
```

```python
from functools import partial
import math

import jax
import jax.numpy as jnp
from jax import lax
from jax.experimental import pallas as pl
from jax.experimental.pallas import tpu as pltpu
from jax.sharding import PartitionSpec as P

GROUPS = 16
CG = 96
RANK = 16
HALF = 8
HALF_LANES = HALF * CG
QUAD = 4
QUAD_LANES = QUAD * CG
ROWS = 9 * CG
PITCH = 32

LEARN = 0.5
MIXING = 0.5
EPSILON = 1e-06
SCALE = 1.0 / math.sqrt(ROWS)
F32 = jnp.float32
BF16 = jnp.bfloat16
LIMIT = 56 * 1024 * 1024


def thirds(value):
    high = value.astype(BF16)
    rest = value - high.astype(F32)
    middle = rest.astype(BF16)
    low = (rest - middle.astype(F32)).astype(BF16)
    return high, middle, low


def contract(left, right, left_dim, right_dim):
    return lax.dot_general(
        left, right, (((left_dim,), (right_dim,)), ((), ())), preferred_element_type=F32
    )


def lane_group(shape):
    return lax.broadcasted_iota(jnp.int32, shape, len(shape) - 1) // CG


def plan_kernel(row_bits, col_bits, step_ref, row_ref, col_ref, level_ref, parity_ref):
    position = lax.rem(step_ref[0], row_ref.shape[0])
    row_offset = row_ref[position]
    col_offset = col_ref[position]
    level = jnp.int32(0)
    for bit in range(row_bits):
        level = level + jnp.where(row_offset > (1 << bit), col_bits, 0)
    for bit in range(col_bits):
        level = level + jnp.where(col_offset > (1 << bit), 1, 0)
    level_ref[0] = level
    side = jnp.bitwise_and(lax.axis_index("row"), row_offset)
    parity_ref[0] = jnp.where(side == 0, jnp.float32(1.0), jnp.float32(-1.0))


def own_lanes():
    shape = (RANK, HALF, HALF_LANES)
    return lane_group(shape) == lax.broadcasted_iota(jnp.int32, shape, 1)


def sketch_kernel(own_ref, peer_ref, weight_ref, error_ref, out_ref):
    warm = ((own_ref[...] + peer_ref[...]) * 0.5).T
    thin = jnp.concatenate(
        [warm[group * RANK : (group + 1) * RANK] for group in range(HALF)], axis=1
    )
    count = RANK * HALF
    spread = jnp.where(own_lanes(), thin[:, None, :], 0.0).reshape(count, HALF_LANES)
    left = jnp.concatenate(thirds(spread), axis=0)
    total = contract(left, weight_ref[...].reshape(ROWS, HALF_LANES), 1, 1)
    total = total + contract(left, error_ref[...].reshape(ROWS, HALF_LANES), 1, 1)
    out_ref[...] = (
        total[:count] + total[count : 2 * count] + total[2 * count :]
    ).reshape(RANK, HALF, ROWS)


def basis_kernel(parity_ref, own_ref, peer_ref, weight_ref, error_ref, basis_ref, proj_ref):
    basis_ref[...] = parity_ref[0] * (own_ref[...] - peer_ref[...])
    for number in range(RANK):
        vector = basis_ref[number]
        norm = jnp.sum(vector * vector, axis=1, keepdims=True)
        vector = vector * lax.rsqrt(norm + EPSILON)
        basis_ref[number] = vector
        for later in range(number + 1, RANK):
            target = basis_ref[later]
            inner = jnp.sum(vector * target, axis=1, keepdims=True)
            basis_ref[later] = target - inner * vector
    count = RANK * HALF
    left = jnp.concatenate(thirds(basis_ref[...].reshape(count, ROWS)), axis=0)
    total = contract(left, weight_ref[...].reshape(ROWS, HALF_LANES), 1, 0)
    total = total + contract(left, error_ref[...].reshape(ROWS, HALF_LANES), 1, 0)
    total = (total[:count] + total[count : 2 * count] + total[2 * count :]).reshape(
        RANK, HALF, HALF_LANES
    )
    proj_ref[...] = jnp.sum(jnp.where(own_lanes(), total, 0.0), axis=1)


def chosen(first_ref, second_ref):
    return jnp.where(pl.program_id(0) == 0, first_ref[...], second_ref[...])


def expand(basis, factor):
    count = RANK * HALF
    own = lane_group((RANK, HALF, HALF_LANES)) == lax.broadcasted_iota(
        jnp.int32, (RANK, HALF, HALF_LANES), 1
    )
    spread = jnp.where(own, factor[:, None, :], 0.0).reshape(count, HALF_LANES)
    high, middle, _ = thirds(basis.reshape(count, ROWS))
    spread_high, spread_middle, _ = thirds(spread)
    left = jnp.concatenate([high, high, middle], axis=0)
    right = jnp.concatenate([spread_high, spread_middle, spread_high], axis=0)
    return contract(left, right, 0, 0)


def errors_kernel(basis0_ref, basis1_ref, proj0_ref, proj1_ref, weight_ref, error_ref, out_ref):
    retained = expand(chosen(basis0_ref, basis1_ref), chosen(proj0_ref, proj1_ref))
    merged = weight_ref[...].astype(F32) + error_ref[...].astype(F32)
    out_ref[...] = (0.5 * MIXING * (merged - retained.reshape(9, CG, HALF_LANES))).astype(BF16)


def weights_kernel(
    parity_ref, basis0_ref, basis1_ref, own0_ref, own1_ref, peer0_ref, peer1_ref, base_ref,
    out_ref, factor_ref,
):
    factor = parity_ref[0] * (chosen(own0_ref, own1_ref) - chosen(peer0_ref, peer1_ref))
    tall = jnp.concatenate(
        [factor[:, group * CG : (group + 1) * CG] for group in range(HALF)], axis=0
    )
    factor_ref[...] = tall.T
    lowrank = expand(chosen(basis0_ref, basis1_ref), factor).reshape(9, CG, HALF_LANES)
    out_ref[...] = (base_ref[...] - 0.5 * MIXING * parity_ref[0] * lowrank).astype(BF16)


def conv_kernel(x_ref, dy_ref, weight_ref, grad_ref, base_ref, x_pad, dy_pad):
    tall, wide, lanes = x_ref.shape
    band = dy_ref.shape[0]
    x_pad[...] = jnp.zeros_like(x_pad)
    dy_pad[...] = jnp.zeros_like(dy_pad)
    x_pad[:, 8 : 8 + wide, :] = x_ref[...].astype(F32)
    dy_pad[:, 8 : 8 + wide, :] = dy_ref[...].astype(F32)
    edge = jnp.zeros((2 * PITCH, lanes), BF16)
    shifted = []
    for lateral in range(3):
        body = dy_pad[:, 9 - lateral : 9 - lateral + PITCH, :].astype(BF16)
        shifted.append(
            jnp.concatenate([edge, body.reshape(band * PITCH, lanes), edge], axis=0)
        )
    count = tall * PITCH

    def lowered(lateral, vertical):
        start = (2 - vertical) * PITCH
        return shifted[lateral][start : start + count]

    upward = jnp.concatenate([lowered(1, vertical) for vertical in range(3)], axis=1)
    groups = lane_group((CG, lanes))
    for lateral in range(3):
        window = x_pad[:, 7 + lateral : 7 + lateral + PITCH, :].astype(BF16)
        result = contract(window.reshape(count, lanes), upward, 0, 0)
        for vertical in range(3):
            tap = 3 * vertical + lateral
            columns = slice(vertical * lanes, (vertical + 1) * lanes)
            gradient = result[:CG, columns]
            for group in range(1, QUAD):
                gradient = jnp.where(
                    groups == group, result[group * CG : (group + 1) * CG, columns], gradient
                )
            base_ref[tap] = weight_ref[tap].astype(F32) - (LEARN * SCALE) * gradient
    total = jnp.zeros((count, lanes), F32)
    zero = jnp.zeros((CG, lanes), BF16)
    for vertical in range(3):
        for lateral in range(3):
            kernel = weight_ref[3 * vertical + lateral]
            blocked = jnp.concatenate(
                [jnp.where(groups == group, kernel, zero) for group in range(QUAD)], axis=0
            )
            total = total + contract(lowered(lateral, vertical), blocked, 1, 1)
    grad_ref[...] = (total * SCALE).reshape(tall, PITCH, lanes)[:, :wide, :].astype(BF16)


def params():
    return pltpu.CompilerParams(vmem_limit_bytes=LIMIT)


SCALAR = pl.BlockSpec(memory_space=pltpu.SMEM)
WHOLE = pl.BlockSpec(memory_space=pltpu.VMEM)
TAPS = pl.BlockSpec((9, CG, HALF_LANES), lambda i: (0, 0, i))
HALF_BASIS = jax.ShapeDtypeStruct((RANK, HALF, ROWS), F32)
HALF_THIN = jax.ShapeDtypeStruct((RANK, HALF_LANES), F32)


def fixed(shape, half=0):
    place = (0,) * (len(shape) - 1) + (half,)
    return pl.BlockSpec(shape, lambda i: place)


def cost(flops, moved):
    return pl.CostEstimate(flops=flops, bytes_accessed=moved, transcendentals=0)


def plan_of(step, row_offsets, col_offsets, row_bits, col_bits):
    return pl.pallas_call(
        partial(plan_kernel, row_bits, col_bits),
        in_specs=[SCALAR] * 3,
        out_specs=(SCALAR, SCALAR),
        out_shape=(jax.ShapeDtypeStruct((1,), jnp.int32), jax.ShapeDtypeStruct((1,), F32)),
    )(step.reshape(1), row_offsets, col_offsets)


def sketch_of(half, own, peer, weights, errors):
    taps = fixed((9, CG, HALF_LANES), half)
    factor = fixed((CG, HALF * RANK), half)
    return pl.pallas_call(
        sketch_kernel,
        grid=(1,),
        in_specs=[factor, factor, taps, taps],
        out_specs=fixed(HALF_BASIS.shape),
        out_shape=HALF_BASIS,
        compiler_params=params(),
        cost_estimate=cost(2 * 10**9, 6 * 10**6),
    )(own, peer, weights, errors)


def basis_of(half, parity, own, peer, weights, errors):
    taps = fixed((9, CG, HALF_LANES), half)
    basis, thin = fixed(HALF_BASIS.shape), fixed(HALF_THIN.shape)
    return pl.pallas_call(
        basis_kernel,
        grid=(1,),
        in_specs=[SCALAR, basis, basis, taps, taps],
        out_specs=(basis, thin),
        out_shape=(HALF_BASIS, HALF_THIN),
        compiler_params=params(),
        cost_estimate=cost(4 * 10**9, 12 * 10**6),
    )(parity, own, peer, weights, errors)


def errors_of(bases, projs, weights, errors):
    basis, thin = fixed(HALF_BASIS.shape), fixed(HALF_THIN.shape)
    return pl.pallas_call(
        errors_kernel,
        grid=(GROUPS // HALF,),
        in_specs=[basis, basis, thin, thin, TAPS, TAPS],
        out_specs=TAPS,
        out_shape=jax.ShapeDtypeStruct(errors.shape, BF16),
        compiler_params=params(),
        cost_estimate=cost(4 * 10**9, 10 * 10**6),
    )(*bases, *projs, weights, errors)


def weights_of(parity, bases, owns, peers, base):
    basis, thin = fixed(HALF_BASIS.shape), fixed(HALF_THIN.shape)
    return pl.pallas_call(
        weights_kernel,
        grid=(GROUPS // HALF,),
        in_specs=[SCALAR, basis, basis, thin, thin, thin, thin, TAPS],
        out_specs=(TAPS, pl.BlockSpec((CG, HALF * RANK), lambda i: (0, i))),
        out_shape=(
            jax.ShapeDtypeStruct(base.shape, BF16),
            jax.ShapeDtypeStruct((CG, GROUPS * RANK), F32),
        ),
        compiler_params=params(),
    )(parity, *bases, *owns, *peers, base)


def conv_of(activations, upstream, weights):
    def banded(rows, wide):
        return pl.BlockSpec((rows, wide, QUAD_LANES), lambda i: (0, 0, i))

    tall, wide, _ = activations.shape
    band = upstream.shape[0]
    taps = pl.BlockSpec((9, CG, QUAD_LANES), lambda i: (0, 0, i))
    return pl.pallas_call(
        conv_kernel,
        grid=(GROUPS // QUAD,),
        in_specs=[banded(tall, wide), banded(band, wide), taps],
        out_specs=(banded(tall, wide), taps),
        out_shape=(
            jax.ShapeDtypeStruct(activations.shape, BF16),
            jax.ShapeDtypeStruct(weights.shape, F32),
        ),
        scratch_shapes=[
            pltpu.VMEM((tall, PITCH + 16, QUAD_LANES), F32),
            pltpu.VMEM((band, PITCH + 16, QUAD_LANES), F32),
        ],
        compiler_params=params(),
        cost_estimate=pl.CostEstimate(
            flops=16 * 10**9, bytes_accessed=12 * 10**6, transcendentals=0
        ),
    )(activations, upstream, weights)


def paired(value, row_bit, col_bit):
    rows, cols = lax.axis_size("row"), lax.axis_size("col")
    pairs = [
        (r * cols + c, (r ^ (1 << row_bit)) * cols + (c ^ (1 << col_bit)))
        for r in range(rows)
        for c in range(cols)
    ]
    return lax.ppermute(value, ("row", "col"), pairs)


def local(activations, grad_out, weights, errors, factors, step, row_offsets, col_offsets):
    row_bits = lax.axis_size("row").bit_length() - 1
    col_bits = lax.axis_size("col").bit_length() - 1
    level, parity = plan_of(step, row_offsets, col_offsets, row_bits, col_bits)

    def whole(row_bit, col_bit, inputs, upstream, taps, carried, own_factor, parity):
        peer_factor = paired(own_factor, row_bit, col_bit)
        first = sketch_of(0, own_factor, peer_factor, taps, carried)
        first_peer = paired(first, row_bit, col_bit)
        second = sketch_of(1, own_factor, peer_factor, taps, carried)
        second_peer = paired(second, row_bit, col_bit)
        inputs, second = lax.optimization_barrier((inputs, second))
        input_grad, base = conv_of(inputs, upstream, taps)
        first_peer, base = lax.optimization_barrier((first_peer, base))
        basis0, own0 = basis_of(0, parity, first, first_peer, taps, carried)
        peer0 = paired(own0, row_bit, col_bit)
        basis1, own1 = basis_of(1, parity, second, second_peer, taps, carried)
        peer1 = paired(own1, row_bit, col_bit)
        bases, owns = (basis0, basis1), (own0, own1)
        next_errors = errors_of(bases, owns, taps, carried)
        next_weights, next_factor = weights_of(parity, bases, owns, (peer0, peer1), base)
        return input_grad, next_weights, next_errors, next_factor

    branches = [
        partial(whole, row_bit, col_bit)
        for row_bit in range(row_bits)
        for col_bit in range(col_bits)
    ]
    results = lax.switch(
        level[0], branches, activations[0], grad_out[0], weights[0], errors[0], factors[0], parity
    )
    return tuple(value[None] for value in results)


def solution(mesh):
    placed = (
        P(("row", "col"), None, None, None),
        P(("row", "col"), None, None, None),
        P(("row", "col"), None, None, None),
        P(("row", "col"), None, None, None),
        P(("row", "col"), None, None),
        P(),
        P(),
        P(),
    )
    return jax.shard_map(
        local,
        mesh=mesh,
        in_specs=placed,
        out_specs=(
            P(("row", "col"), None, None, None),
            P(("row", "col"), None, None, None),
            P(("row", "col"), None, None, None),
            P(("row", "col"), None, None),
        ),
        check_vma=False,
    )
```

```python
from functools import partial
import math

import jax
import jax.numpy as jnp
from jax import lax
from jax.experimental import pallas as pl
from jax.experimental.pallas import tpu as pltpu
from jax.sharding import PartitionSpec as P

GROUPS = 16
CG = 96
RANK = 16
HALF = 8
HALF_LANES = HALF * CG
QUAD = 4
QUAD_LANES = QUAD * CG
ROWS = 9 * CG
PITCH = 32

LEARN = 0.5
MIXING = 0.5
EPSILON = 1e-06
SCALE = 1.0 / math.sqrt(ROWS)
F32 = jnp.float32
BF16 = jnp.bfloat16
LIMIT = 56 * 1024 * 1024


def thirds(value):
    high = value.astype(BF16)
    rest = value - high.astype(F32)
    middle = rest.astype(BF16)
    low = (rest - middle.astype(F32)).astype(BF16)
    return high, middle, low


def contract(left, right, left_dim, right_dim):
    return lax.dot_general(
        left, right, (((left_dim,), (right_dim,)), ((), ())), preferred_element_type=F32
    )


def lane_group(shape):
    return lax.broadcasted_iota(jnp.int32, shape, len(shape) - 1) // CG


def plan_kernel(row_bits, col_bits, step_ref, row_ref, col_ref, level_ref, parity_ref):
    position = lax.rem(step_ref[0], row_ref.shape[0])
    row_offset = row_ref[position]
    col_offset = col_ref[position]
    level = jnp.int32(0)
    for bit in range(row_bits):
        level = level + jnp.where(row_offset > (1 << bit), col_bits, 0)
    for bit in range(col_bits):
        level = level + jnp.where(col_offset > (1 << bit), 1, 0)
    level_ref[0] = level
    side = jnp.bitwise_and(lax.axis_index("row"), row_offset)
    parity_ref[0] = jnp.where(side == 0, jnp.float32(1.0), jnp.float32(-1.0))


def own_lanes():
    shape = (RANK, HALF, HALF_LANES)
    return lane_group(shape) == lax.broadcasted_iota(jnp.int32, shape, 1)


def sketch_kernel(own_ref, peer_ref, weight_ref, error_ref, out_ref):
    warm = ((own_ref[...] + peer_ref[...]) * 0.5).T
    thin = jnp.concatenate(
        [warm[group * RANK : (group + 1) * RANK] for group in range(HALF)], axis=1
    )
    count = RANK * HALF
    spread = jnp.where(own_lanes(), thin[:, None, :], 0.0).reshape(count, HALF_LANES)
    left = jnp.concatenate(thirds(spread), axis=0)
    total = contract(left, weight_ref[...].reshape(ROWS, HALF_LANES), 1, 1)
    total = total + contract(left, error_ref[...].reshape(ROWS, HALF_LANES), 1, 1)
    out_ref[...] = (
        total[:count] + total[count : 2 * count] + total[2 * count :]
    ).reshape(RANK, HALF, ROWS)


def basis_kernel(parity_ref, own_ref, peer_ref, weight_ref, error_ref, basis_ref, proj_ref):
    basis_ref[...] = parity_ref[0] * (own_ref[...] - peer_ref[...])
    for number in range(RANK):
        vector = basis_ref[number]
        norm = jnp.sum(vector * vector, axis=1, keepdims=True)
        vector = vector * lax.rsqrt(norm + EPSILON)
        basis_ref[number] = vector
        for later in range(number + 1, RANK):
            target = basis_ref[later]
            inner = jnp.sum(vector * target, axis=1, keepdims=True)
            basis_ref[later] = target - inner * vector
    count = RANK * HALF
    for half in range(GROUPS // HALF):
        lanes = slice(half * HALF_LANES, (half + 1) * HALF_LANES)
        part = basis_ref[:, half * HALF : (half + 1) * HALF, :].reshape(count, ROWS)
        left = jnp.concatenate(thirds(part), axis=0)
        total = contract(left, weight_ref[:, :, lanes].reshape(ROWS, HALF_LANES), 1, 0)
        total = total + contract(left, error_ref[:, :, lanes].reshape(ROWS, HALF_LANES), 1, 0)
        total = (total[:count] + total[count : 2 * count] + total[2 * count :]).reshape(
            RANK, HALF, HALF_LANES
        )
        own = lane_group((RANK, HALF, HALF_LANES)) == lax.broadcasted_iota(
            jnp.int32, (RANK, HALF, HALF_LANES), 1
        )
        proj_ref[:, lanes] = jnp.sum(jnp.where(own, total, 0.0), axis=1)


def expand(basis, factor):
    count = RANK * HALF
    own = lane_group((RANK, HALF, HALF_LANES)) == lax.broadcasted_iota(
        jnp.int32, (RANK, HALF, HALF_LANES), 1
    )
    spread = jnp.where(own, factor[:, None, :], 0.0).reshape(count, HALF_LANES)
    high, middle, _ = thirds(basis.reshape(count, ROWS))
    spread_high, spread_middle, _ = thirds(spread)
    left = jnp.concatenate([high, high, middle], axis=0)
    right = jnp.concatenate([spread_high, spread_middle, spread_high], axis=0)
    return contract(left, right, 0, 0)


def errors_kernel(basis_ref, proj_ref, weight_ref, error_ref, out_ref):
    retained = expand(basis_ref[...], proj_ref[...]).reshape(9, CG, HALF_LANES)
    merged = weight_ref[...].astype(F32) + error_ref[...].astype(F32)
    out_ref[...] = (0.5 * MIXING * (merged - retained)).astype(BF16)


def weights_kernel(parity_ref, basis_ref, own_ref, peer_ref, base_ref, out_ref, factor_ref):
    factor = parity_ref[0] * (own_ref[...] - peer_ref[...])
    tall = jnp.concatenate(
        [factor[:, group * CG : (group + 1) * CG] for group in range(HALF)], axis=0
    )
    factor_ref[...] = tall.T
    lowrank = expand(basis_ref[...], factor).reshape(9, CG, HALF_LANES)
    out_ref[...] = (base_ref[...] - 0.5 * MIXING * parity_ref[0] * lowrank).astype(BF16)


def conv_kernel(x_ref, dy_ref, weight_ref, grad_ref, base_ref, x_pad, dy_pad):
    tall, wide, lanes = x_ref.shape
    band = dy_ref.shape[0]
    x_pad[...] = jnp.zeros_like(x_pad)
    dy_pad[...] = jnp.zeros_like(dy_pad)
    x_pad[:, 8 : 8 + wide, :] = x_ref[...].astype(F32)
    dy_pad[:, 8 : 8 + wide, :] = dy_ref[...].astype(F32)
    edge = jnp.zeros((2 * PITCH, lanes), BF16)
    shifted = []
    for lateral in range(3):
        body = dy_pad[:, 9 - lateral : 9 - lateral + PITCH, :].astype(BF16)
        shifted.append(
            jnp.concatenate([edge, body.reshape(band * PITCH, lanes), edge], axis=0)
        )
    count = tall * PITCH

    def lowered(lateral, vertical):
        start = (2 - vertical) * PITCH
        return shifted[lateral][start : start + count]

    upward = jnp.concatenate([lowered(1, vertical) for vertical in range(3)], axis=1)
    groups = lane_group((CG, lanes))
    for lateral in range(3):
        window = x_pad[:, 7 + lateral : 7 + lateral + PITCH, :].astype(BF16)
        result = contract(window.reshape(count, lanes), upward, 0, 0)
        for vertical in range(3):
            tap = 3 * vertical + lateral
            columns = slice(vertical * lanes, (vertical + 1) * lanes)
            gradient = result[:CG, columns]
            for group in range(1, QUAD):
                gradient = jnp.where(
                    groups == group, result[group * CG : (group + 1) * CG, columns], gradient
                )
            base_ref[tap] = weight_ref[tap].astype(F32) - (LEARN * SCALE) * gradient
    total = jnp.zeros((count, lanes), F32)
    zero = jnp.zeros((CG, lanes), BF16)
    for vertical in range(3):
        for lateral in range(3):
            kernel = weight_ref[3 * vertical + lateral]
            blocked = jnp.concatenate(
                [jnp.where(groups == group, kernel, zero) for group in range(QUAD)], axis=0
            )
            total = total + contract(lowered(lateral, vertical), blocked, 1, 1)
    grad_ref[...] = (total * SCALE).reshape(tall, PITCH, lanes)[:, :wide, :].astype(BF16)


def params():
    return pltpu.CompilerParams(vmem_limit_bytes=LIMIT)


SCALAR = pl.BlockSpec(memory_space=pltpu.SMEM)
WHOLE = pl.BlockSpec(memory_space=pltpu.VMEM)
TAPS = pl.BlockSpec((9, CG, HALF_LANES), lambda i: (0, 0, i))
BASIS = pl.BlockSpec((RANK, HALF, ROWS), lambda i: (0, i, 0))
FACTOR = pl.BlockSpec((CG, HALF * RANK), lambda i: (0, i))
THIN = pl.BlockSpec((RANK, HALF_LANES), lambda i: (0, i))


def plan_of(step, row_offsets, col_offsets, row_bits, col_bits):
    return pl.pallas_call(
        partial(plan_kernel, row_bits, col_bits),
        in_specs=[SCALAR] * 3,
        out_specs=(SCALAR, SCALAR),
        out_shape=(jax.ShapeDtypeStruct((1,), jnp.int32), jax.ShapeDtypeStruct((1,), F32)),
    )(step.reshape(1), row_offsets, col_offsets)


def sketch_of(own, peer, weights, errors):
    return pl.pallas_call(
        sketch_kernel,
        grid=(GROUPS // HALF,),
        in_specs=[FACTOR, FACTOR, TAPS, TAPS],
        out_specs=BASIS,
        out_shape=jax.ShapeDtypeStruct((RANK, GROUPS, ROWS), F32),
        compiler_params=params(),
    )(own, peer, weights, errors)


def basis_of(parity, own, peer, weights, errors):
    return pl.pallas_call(
        basis_kernel,
        in_specs=[SCALAR, WHOLE, WHOLE, WHOLE, WHOLE],
        out_specs=(WHOLE, WHOLE),
        out_shape=(
            jax.ShapeDtypeStruct((RANK, GROUPS, ROWS), F32),
            jax.ShapeDtypeStruct((RANK, GROUPS * CG), F32),
        ),
        compiler_params=params(),
    )(parity, own, peer, weights, errors)


def errors_of(basis, proj, weights, errors):
    return pl.pallas_call(
        errors_kernel,
        grid=(GROUPS // HALF,),
        in_specs=[BASIS, THIN, TAPS, TAPS],
        out_specs=TAPS,
        out_shape=jax.ShapeDtypeStruct(errors.shape, BF16),
        compiler_params=params(),
        cost_estimate=pl.CostEstimate(
            flops=4 * 10**9, bytes_accessed=10 * 10**6, transcendentals=0
        ),
    )(basis, proj, weights, errors)


def weights_of(parity, basis, own, peer, base):
    return pl.pallas_call(
        weights_kernel,
        grid=(GROUPS // HALF,),
        in_specs=[SCALAR, BASIS, THIN, THIN, TAPS],
        out_specs=(TAPS, FACTOR),
        out_shape=(
            jax.ShapeDtypeStruct(base.shape, BF16),
            jax.ShapeDtypeStruct((CG, GROUPS * RANK), F32),
        ),
        compiler_params=params(),
    )(parity, basis, own, peer, base)


def conv_of(activations, upstream, weights):
    def banded(rows, wide):
        return pl.BlockSpec((rows, wide, QUAD_LANES), lambda i: (0, 0, i))

    tall, wide, _ = activations.shape
    band = upstream.shape[0]
    taps = pl.BlockSpec((9, CG, QUAD_LANES), lambda i: (0, 0, i))
    return pl.pallas_call(
        conv_kernel,
        grid=(GROUPS // QUAD,),
        in_specs=[banded(tall, wide), banded(band, wide), taps],
        out_specs=(banded(tall, wide), taps),
        out_shape=(
            jax.ShapeDtypeStruct(activations.shape, BF16),
            jax.ShapeDtypeStruct(weights.shape, F32),
        ),
        scratch_shapes=[
            pltpu.VMEM((tall, PITCH + 16, QUAD_LANES), F32),
            pltpu.VMEM((band, PITCH + 16, QUAD_LANES), F32),
        ],
        compiler_params=params(),
        cost_estimate=pl.CostEstimate(
            flops=16 * 10**9, bytes_accessed=12 * 10**6, transcendentals=0
        ),
    )(activations, upstream, weights)


def paired(value, row_bit, col_bit):
    rows, cols = lax.axis_size("row"), lax.axis_size("col")
    pairs = [
        (r * cols + c, (r ^ (1 << row_bit)) * cols + (c ^ (1 << col_bit)))
        for r in range(rows)
        for c in range(cols)
    ]
    return lax.ppermute(value, ("row", "col"), pairs)


def local(activations, grad_out, weights, errors, factors, step, row_offsets, col_offsets):
    row_bits = lax.axis_size("row").bit_length() - 1
    col_bits = lax.axis_size("col").bit_length() - 1
    level, parity = plan_of(step, row_offsets, col_offsets, row_bits, col_bits)

    def across(work, *operands):
        branches = [
            partial(work, lambda value, r=r, c=c: paired(value, r, c))
            for r in range(row_bits)
            for c in range(col_bits)
        ]
        return lax.switch(level[0], branches, *operands)

    taps, carried = weights[0], errors[0]
    own_factor = factors[0]
    peer_factor = across(lambda send, value: send(value), own_factor)
    sketch = sketch_of(own_factor, peer_factor, taps, carried)

    def swap_sketch(send, value, inputs, upstream, kernel):
        return send(value), conv_of(inputs, upstream, kernel)

    remote, (input_grad, base) = across(
        swap_sketch, sketch, activations[0], grad_out[0], taps
    )
    basis, own_proj = basis_of(parity, sketch, remote, taps, carried)

    def swap_proj(send, value, basis, kernel, carried):
        return send(value), errors_of(basis, value, kernel, carried)

    peer_proj, next_errors = across(swap_proj, own_proj, basis, taps, carried)
    next_weights, next_factor = weights_of(parity, basis, own_proj, peer_proj, base)
    return (input_grad[None], next_weights[None], next_errors[None], next_factor[None])


def solution(mesh):
    placed = (
        P(("row", "col"), None, None, None),
        P(("row", "col"), None, None, None),
        P(("row", "col"), None, None, None),
        P(("row", "col"), None, None, None),
        P(("row", "col"), None, None),
        P(),
        P(),
        P(),
    )
    return jax.shard_map(
        local,
        mesh=mesh,
        in_specs=placed,
        out_specs=(
            P(("row", "col"), None, None, None),
            P(("row", "col"), None, None, None),
            P(("row", "col"), None, None, None),
            P(("row", "col"), None, None),
        ),
        check_vma=False,
    )
```

```python
from functools import partial
import math

import jax
import jax.numpy as jnp
from jax import lax
from jax.experimental import pallas as pl
from jax.experimental.pallas import tpu as pltpu
from jax.sharding import PartitionSpec as P

GROUPS = 16
CG = 96
RANK = 16
HALF = 8
HALF_LANES = HALF * CG
QUAD = 4
QUAD_LANES = QUAD * CG
ROWS = 9 * CG
PITCH = 32

LEARN = 0.5
MIXING = 0.5
EPSILON = 1e-06
SCALE = 1.0 / math.sqrt(ROWS)
F32 = jnp.float32
BF16 = jnp.bfloat16
LIMIT = 56 * 1024 * 1024


def thirds(value):
    high = value.astype(BF16)
    rest = value - high.astype(F32)
    middle = rest.astype(BF16)
    low = (rest - middle.astype(F32)).astype(BF16)
    return high, middle, low


def contract(left, right, left_dim, right_dim):
    return lax.dot_general(
        left, right, (((left_dim,), (right_dim,)), ((), ())), preferred_element_type=F32
    )


def lane_group(shape):
    return lax.broadcasted_iota(jnp.int32, shape, len(shape) - 1) // CG


def plan_kernel(row_bits, col_bits, step_ref, row_ref, col_ref, level_ref, parity_ref):
    position = lax.rem(step_ref[0], row_ref.shape[0])
    row_offset = row_ref[position]
    col_offset = col_ref[position]
    level = jnp.int32(0)
    for bit in range(row_bits):
        level = level + jnp.where(row_offset > (1 << bit), col_bits, 0)
    for bit in range(col_bits):
        level = level + jnp.where(col_offset > (1 << bit), 1, 0)
    level_ref[0] = level
    side = jnp.bitwise_and(lax.axis_index("row"), row_offset)
    parity_ref[0] = jnp.where(side == 0, jnp.float32(1.0), jnp.float32(-1.0))


def own_lanes():
    shape = (RANK, HALF, HALF_LANES)
    return lane_group(shape) == lax.broadcasted_iota(jnp.int32, shape, 1)


def sketch_kernel(own_ref, peer_ref, weight_ref, error_ref, out_ref):
    warm = ((own_ref[...] + peer_ref[...]) * 0.5).T
    thin = jnp.concatenate(
        [warm[group * RANK : (group + 1) * RANK] for group in range(HALF)], axis=1
    )
    count = RANK * HALF
    spread = jnp.where(own_lanes(), thin[:, None, :], 0.0).reshape(count, HALF_LANES)
    left = jnp.concatenate(thirds(spread), axis=0)
    total = contract(left, weight_ref[...].reshape(ROWS, HALF_LANES), 1, 1)
    total = total + contract(left, error_ref[...].reshape(ROWS, HALF_LANES), 1, 1)
    out_ref[...] = (
        total[:count] + total[count : 2 * count] + total[2 * count :]
    ).reshape(RANK, HALF, ROWS)


def basis_kernel(parity_ref, own_ref, peer_ref, weight_ref, error_ref, basis_ref, proj_ref):
    basis_ref[...] = parity_ref[0] * (own_ref[...] - peer_ref[...])
    for number in range(RANK):
        vector = basis_ref[number]
        norm = jnp.sum(vector * vector, axis=1, keepdims=True)
        vector = vector * lax.rsqrt(norm + EPSILON)
        basis_ref[number] = vector
        for later in range(number + 1, RANK):
            target = basis_ref[later]
            inner = jnp.sum(vector * target, axis=1, keepdims=True)
            basis_ref[later] = target - inner * vector
    count = RANK * HALF
    for half in range(GROUPS // HALF):
        lanes = slice(half * HALF_LANES, (half + 1) * HALF_LANES)
        part = basis_ref[:, half * HALF : (half + 1) * HALF, :].reshape(count, ROWS)
        left = jnp.concatenate(thirds(part), axis=0)
        total = contract(left, weight_ref[:, :, lanes].reshape(ROWS, HALF_LANES), 1, 0)
        total = total + contract(left, error_ref[:, :, lanes].reshape(ROWS, HALF_LANES), 1, 0)
        total = (total[:count] + total[count : 2 * count] + total[2 * count :]).reshape(
            RANK, HALF, HALF_LANES
        )
        own = lane_group((RANK, HALF, HALF_LANES)) == lax.broadcasted_iota(
            jnp.int32, (RANK, HALF, HALF_LANES), 1
        )
        proj_ref[:, lanes] = jnp.sum(jnp.where(own, total, 0.0), axis=1)


def expand(basis, factor):
    count = RANK * HALF
    own = lane_group((RANK, HALF, HALF_LANES)) == lax.broadcasted_iota(
        jnp.int32, (RANK, HALF, HALF_LANES), 1
    )
    spread = jnp.where(own, factor[:, None, :], 0.0).reshape(count, HALF_LANES)
    high, middle, _ = thirds(basis.reshape(count, ROWS))
    spread_high, spread_middle, _ = thirds(spread)
    left = jnp.concatenate([high, high, middle], axis=0)
    right = jnp.concatenate([spread_high, spread_middle, spread_high], axis=0)
    return contract(left, right, 0, 0)


def errors_kernel(basis_ref, proj_ref, weight_ref, error_ref, out_ref):
    retained = expand(basis_ref[...], proj_ref[...]).reshape(9, CG, HALF_LANES)
    merged = weight_ref[...].astype(F32) + error_ref[...].astype(F32)
    out_ref[...] = (0.5 * MIXING * (merged - retained)).astype(BF16)


def weights_kernel(parity_ref, basis_ref, own_ref, peer_ref, base_ref, out_ref, factor_ref):
    factor = parity_ref[0] * (own_ref[...] - peer_ref[...])
    tall = jnp.concatenate(
        [factor[:, group * CG : (group + 1) * CG] for group in range(HALF)], axis=0
    )
    factor_ref[...] = tall.T
    lowrank = expand(basis_ref[...], factor).reshape(9, CG, HALF_LANES)
    out_ref[...] = (base_ref[...] - 0.5 * MIXING * parity_ref[0] * lowrank).astype(BF16)


def conv_kernel(x_ref, dy_ref, weight_ref, grad_ref, base_ref, x_pad, dy_pad):
    tall, wide, lanes = x_ref.shape
    band = dy_ref.shape[1]
    x_pad[...] = jnp.zeros_like(x_pad)
    dy_pad[...] = jnp.zeros_like(dy_pad)
    x_pad[:, 8 : 8 + wide, :] = x_ref[...].astype(F32)
    for column in range(wide):
        dy_pad[:, 8 + column, :] = dy_ref[column].astype(F32)
    edge = jnp.zeros((2 * PITCH, lanes), BF16)
    shifted = []
    for lateral in range(3):
        body = dy_pad[:, 9 - lateral : 9 - lateral + PITCH, :].astype(BF16)
        shifted.append(
            jnp.concatenate([edge, body.reshape(band * PITCH, lanes), edge], axis=0)
        )
    count = tall * PITCH

    def lowered(lateral, vertical):
        start = (2 - vertical) * PITCH
        return shifted[lateral][start : start + count]

    upward = jnp.concatenate([lowered(1, vertical) for vertical in range(3)], axis=1)
    groups = lane_group((CG, lanes))
    for lateral in range(3):
        window = x_pad[:, 7 + lateral : 7 + lateral + PITCH, :].astype(BF16)
        result = contract(window.reshape(count, lanes), upward, 0, 0)
        for vertical in range(3):
            tap = 3 * vertical + lateral
            columns = slice(vertical * lanes, (vertical + 1) * lanes)
            gradient = result[:CG, columns]
            for group in range(1, QUAD):
                gradient = jnp.where(
                    groups == group, result[group * CG : (group + 1) * CG, columns], gradient
                )
            base_ref[tap] = weight_ref[tap].astype(F32) - (LEARN * SCALE) * gradient
    total = jnp.zeros((count, lanes), F32)
    zero = jnp.zeros((CG, lanes), BF16)
    for vertical in range(3):
        for lateral in range(3):
            kernel = weight_ref[3 * vertical + lateral]
            blocked = jnp.concatenate(
                [jnp.where(groups == group, kernel, zero) for group in range(QUAD)], axis=0
            )
            total = total + contract(lowered(lateral, vertical), blocked, 1, 1)
    grad_ref[...] = (total * SCALE).reshape(tall, PITCH, lanes)[:, :wide, :].astype(BF16)


def params():
    return pltpu.CompilerParams(vmem_limit_bytes=LIMIT)


SCALAR = pl.BlockSpec(memory_space=pltpu.SMEM)
WHOLE = pl.BlockSpec(memory_space=pltpu.VMEM)
TAPS = pl.BlockSpec((9, CG, HALF_LANES), lambda i: (0, 0, i))
BASIS = pl.BlockSpec((RANK, HALF, ROWS), lambda i: (0, i, 0))
FACTOR = pl.BlockSpec((CG, HALF * RANK), lambda i: (0, i))
THIN = pl.BlockSpec((RANK, HALF_LANES), lambda i: (0, i))


def plan_of(step, row_offsets, col_offsets, row_bits, col_bits):
    return pl.pallas_call(
        partial(plan_kernel, row_bits, col_bits),
        in_specs=[SCALAR] * 3,
        out_specs=(SCALAR, SCALAR),
        out_shape=(jax.ShapeDtypeStruct((1,), jnp.int32), jax.ShapeDtypeStruct((1,), F32)),
    )(step.reshape(1), row_offsets, col_offsets)


def sketch_of(own, peer, weights, errors):
    return pl.pallas_call(
        sketch_kernel,
        grid=(GROUPS // HALF,),
        in_specs=[FACTOR, FACTOR, TAPS, TAPS],
        out_specs=BASIS,
        out_shape=jax.ShapeDtypeStruct((RANK, GROUPS, ROWS), F32),
        compiler_params=params(),
    )(own, peer, weights, errors)


def basis_of(parity, own, peer, weights, errors):
    return pl.pallas_call(
        basis_kernel,
        in_specs=[SCALAR, WHOLE, WHOLE, WHOLE, WHOLE],
        out_specs=(WHOLE, WHOLE),
        out_shape=(
            jax.ShapeDtypeStruct((RANK, GROUPS, ROWS), F32),
            jax.ShapeDtypeStruct((RANK, GROUPS * CG), F32),
        ),
        compiler_params=params(),
    )(parity, own, peer, weights, errors)


def errors_of(basis, proj, weights, errors):
    return pl.pallas_call(
        errors_kernel,
        grid=(GROUPS // HALF,),
        in_specs=[BASIS, THIN, TAPS, TAPS],
        out_specs=TAPS,
        out_shape=jax.ShapeDtypeStruct(errors.shape, BF16),
        compiler_params=params(),
        cost_estimate=pl.CostEstimate(
            flops=4 * 10**9, bytes_accessed=10 * 10**6, transcendentals=0
        ),
    )(basis, proj, weights, errors)


def weights_of(parity, basis, own, peer, base):
    return pl.pallas_call(
        weights_kernel,
        grid=(GROUPS // HALF,),
        in_specs=[SCALAR, BASIS, THIN, THIN, TAPS],
        out_specs=(TAPS, FACTOR),
        out_shape=(
            jax.ShapeDtypeStruct(base.shape, BF16),
            jax.ShapeDtypeStruct((CG, GROUPS * RANK), F32),
        ),
        compiler_params=params(),
    )(parity, basis, own, peer, base)


def conv_of(activations, upstream, weights):
    def banded(rows, wide):
        return pl.BlockSpec((rows, wide, QUAD_LANES), lambda i: (0, 0, i))

    tall, wide, _ = activations.shape
    band = upstream.shape[1]
    taps = pl.BlockSpec((9, CG, QUAD_LANES), lambda i: (0, 0, i))
    return pl.pallas_call(
        conv_kernel,
        grid=(GROUPS // QUAD,),
        in_specs=[banded(tall, wide), pl.BlockSpec((wide, band, QUAD_LANES), lambda i: (0, 0, i)), taps],
        out_specs=(banded(tall, wide), taps),
        out_shape=(
            jax.ShapeDtypeStruct(activations.shape, BF16),
            jax.ShapeDtypeStruct(weights.shape, F32),
        ),
        scratch_shapes=[
            pltpu.VMEM((tall, PITCH + 16, QUAD_LANES), F32),
            pltpu.VMEM((band, PITCH + 16, QUAD_LANES), F32),
        ],
        compiler_params=params(),
        cost_estimate=pl.CostEstimate(
            flops=16 * 10**9, bytes_accessed=12 * 10**6, transcendentals=0
        ),
    )(activations, upstream, weights)


def paired(value, row_bit, col_bit):
    rows, cols = lax.axis_size("row"), lax.axis_size("col")
    pairs = [
        (r * cols + c, (r ^ (1 << row_bit)) * cols + (c ^ (1 << col_bit)))
        for r in range(rows)
        for c in range(cols)
    ]
    return lax.ppermute(value, ("row", "col"), pairs)


def local(activations, grad_out, weights, errors, factors, step, row_offsets, col_offsets):
    row_bits = lax.axis_size("row").bit_length() - 1
    col_bits = lax.axis_size("col").bit_length() - 1
    level, parity = plan_of(step, row_offsets, col_offsets, row_bits, col_bits)

    def across(work, *operands):
        branches = [
            partial(work, lambda value, r=r, c=c: paired(value, r, c))
            for r in range(row_bits)
            for c in range(col_bits)
        ]
        return lax.switch(level[0], branches, *operands)

    taps, carried = weights[0], errors[0]
    own_factor = factors[0]
    peer_factor = across(lambda send, value: send(value), own_factor)
    sketch = sketch_of(own_factor, peer_factor, taps, carried)

    def swap_sketch(send, value, inputs, upstream, kernel):
        return send(value), conv_of(inputs, upstream, kernel)

    remote, (input_grad, base) = across(
        swap_sketch, sketch, activations[0], grad_out[0].transpose(1, 0, 2), taps
    )
    basis, own_proj = basis_of(parity, sketch, remote, taps, carried)

    def swap_proj(send, value, basis, kernel, carried):
        return send(value), errors_of(basis, value, kernel, carried)

    peer_proj, next_errors = across(swap_proj, own_proj, basis, taps, carried)
    next_weights, next_factor = weights_of(parity, basis, own_proj, peer_proj, base)
    return (input_grad[None], next_weights[None], next_errors[None], next_factor[None])


def solution(mesh):
    placed = (
        P(("row", "col"), None, None, None),
        P(("row", "col"), None, None, None),
        P(("row", "col"), None, None, None),
        P(("row", "col"), None, None, None),
        P(("row", "col"), None, None),
        P(),
        P(),
        P(),
    )
    return jax.shard_map(
        local,
        mesh=mesh,
        in_specs=placed,
        out_specs=(
            P(("row", "col"), None, None, None),
            P(("row", "col"), None, None, None),
            P(("row", "col"), None, None, None),
            P(("row", "col"), None, None),
        ),
        check_vma=False,
    )
```
